256 devices in a mesh: dp: 16 (over y_hi, x, core), ctx: 16 (over y_lo, z).
Axes of the slice: x: 4, y: 4 (y_hi: 2, y_lo: 2; y = y_hi * 2 + y_lo), z: 8, core: 2. Of those that a mesh axis runs over, the one named last changes fastest.
Arguments:
- queries: bfloat16 [16, 2048, 2048], P('dp', 'ctx'), may hold values from -8 to 8, as said below
- key_rows: bfloat16 [16, 2048, 2048], P('dp', 'ctx'), may hold values from -8 to 8, as said below
- value_rows: bfloat16 [16, 2048, 2048], P('dp', 'ctx'), may hold values from -6 to 6
- reflections: bfloat16 [16, 2048, 2048], P('dp', 'ctx'), may hold values from -8 to 8, as said below
- segment_ids: int32 [16, 2048], P('dp', 'ctx'), may hold values from 0 to 7, never falling along the last dimension, each value on 1 to 1024 neighbouring positions
- head_gains: float32 [2048], P('dp'), may hold values from 0.1 to 1.9
Outputs:
- attended_out: bfloat16 [16, 2048, 2048], P('dp', 'ctx')
The draws below stay inside these ranges and needn't reach their ends.
Inputs may be any that keep to these rules, and one draw needn't show every extreme that they name: queries of order one. `key_rows`: keys of order one. `reflections`: every row has nonzero entries in every head. `segment_ids`: document numbers never fall along a sequence; one document has exactly 1024 positions.
All inputs are finite; a program needn't handle non-finite values.
Results may differ from the reference program's by a relative error of at most 0.0097.
Values may be sent and summed in bfloat16 or wider, within the bound.
A program may use at most 128 MiB of HBM per device.

```python
import math
import jax
import jax.numpy as jnp
import numpy as np
from jax import lax

HEADS = 16
HD = 128
BLK = 64
DOCS = 8
LENGTH = 2048
SEQS = 16


def draw_queries(key, part):
    key = jax.random.fold_in(key, 11)
    return jnp.clip(1.5 * jax.random.normal(key, (SEQS, LENGTH, HEADS * HD)), -8.0, 8.0).astype(jnp.bfloat16)


def draw_key_rows(key, part):
    key = jax.random.fold_in(key, 12)
    return jnp.clip(1.5 * jax.random.normal(key, (SEQS, LENGTH, HEADS * HD)), -8.0, 8.0).astype(jnp.bfloat16)


def draw_reflections(key, part):
    key = jax.random.fold_in(key, 13)
    return jnp.clip(jax.random.normal(key, (SEQS, LENGTH, HEADS * HD)), -8.0, 8.0).astype(jnp.bfloat16)


def block_scale(stream_key, dims, shards, smallest, high):
    def one(axis_at, parts):
        steps = jax.random.uniform(jax.random.fold_in(jax.random.fold_in(stream_key, 6), axis_at), (parts,), jnp.float32, smallest / len(shards), high / len(shards))
        return jnp.repeat(jnp.exp(steps), dims[axis_at] // parts).reshape((-1,) + (1,) * (len(dims) - axis_at - 1))

    gain = one(*shards[0])
    for cut in shards[1:]:
        gain = gain * one(*cut)
    return gain


def split_up(count, total, limit, slope):
    loads = [(1 << 20) // math.isqrt(standing ** slope) + 1 for standing in range(2, count + 1)]
    surplus, holding = total - limit - (count - 1), [1] * (count - 1)
    while surplus > 0:
        movable = [i for i in range(count - 1) if holding[i] < limit]
        mass, budget = sum([loads[i] for i in movable]), surplus
        for i in movable:
            extra = min(limit - holding[i], max(1, budget * loads[i] // mass), surplus)
            holding[i] = holding[i] + extra
            surplus = surplus - extra
    return np.array([limit] + holding)


def uneven_parts(key, count, total, limit, slope):
    if count == 2:
        one = jax.random.randint(key, (), max(1, total - limit), min(limit, total - 1) + 1)
        return jnp.stack([one, total - one])
    lengths = jnp.asarray(split_up(count, total, limit, slope), jnp.int32)
    couples = (count - 1) // 2
    giver, sink = lengths[1:1 + 2 * couples:2], lengths[2:2 + 2 * couples:2]
    slack = jnp.minimum(giver - 1, limit - sink)
    passed = jax.random.randint(jax.random.fold_in(key, 1), (couples,), 0, 1 << 20) % (slack + 1)
    lengths = lengths.at[1:1 + 2 * couples:2].set(giver - passed).at[2:2 + 2 * couples:2].set(sink + passed)
    return lengths[jax.random.permutation(jax.random.fold_in(key, 2), count)]


def normal_values(stream_key, extent, deviation, limit, pieces=(), kind=jnp.bfloat16):
    loudness = block_scale(stream_key, extent, pieces, -0.22, 0.18) if pieces else 1.0
    drawn = jax.random.normal(stream_key, extent, jnp.float32) * deviation * loudness
    return jnp.minimum(jnp.maximum(drawn, -limit), limit).astype(kind)


def setup_inputs(seed: int = 0) -> dict:
    key_list = jax.random.split(jax.random.key(seed), 7)
    return {
        "queries": draw_queries(jax.random.fold_in(key_list[6], 71), 0),
        "key_rows": draw_key_rows(jax.random.fold_in(key_list[6], 71), 0),
        "value_rows": normal_values(key_list[2], (SEQS, LENGTH, HEADS * HD), 1.0, 6.0, ((0, 16), (1, 16))),
        "reflections": draw_reflections(jax.random.fold_in(key_list[6], 71), 0),
        "segment_ids": jax.vmap(lambda own: jnp.searchsorted(jnp.cumsum(uneven_parts(own, DOCS, LENGTH, LENGTH // 2, 2)), jnp.arange(LENGTH), side="right"))(jax.random.split(key_list[4], SEQS)).reshape((SEQS, LENGTH)).astype(jnp.int32),
        "head_gains": jnp.clip(1.0 + 0.18 * jax.random.normal(key_list[5], (HEADS * HD,), jnp.float32), 0.1, 1.9),
    }


epsilon = 1e-06
neg_large = -1e+30
highest = lax.Precision.HIGHEST

def normalized(raw_rows):
    floats = raw_rows.astype(jnp.float32)
    return floats * lax.rsqrt(lax.optimization_barrier(jnp.sum(floats * floats, axis=-1, keepdims=True)) + epsilon)

def upper_inverse(strict_upper):
    block_size = strict_upper.shape[0]
    eye_block = jnp.eye(block_size, dtype=jnp.float32)
    power = -2.0 * strict_upper
    result = eye_block + power
    covered = 2
    while covered < block_size:
        power = jnp.dot(power, power, precision=highest)
        result = jnp.dot(result, eye_block + power, precision=highest)
        covered = covered * 2
    return 2.0 * result

def block_terms(vectors, query_part, key_part):
    block_size = vectors.shape[0]
    feature_width = vectors.shape[1]
    gram_matrix = jnp.dot(vectors, vectors.T, precision=highest)
    inverse = upper_inverse(jnp.triu(gram_matrix, 1))
    upper_mask = jnp.triu(jnp.ones((block_size, block_size), jnp.float32))
    query_terms = jnp.dot(vectors, query_part.T, precision=highest) * upper_mask
    key_terms = jnp.dot(vectors, key_part.T, precision=highest) * upper_mask
    stacked = jnp.concatenate([query_terms, key_terms, vectors], axis=1)
    solved = jnp.dot(inverse, stacked, precision=highest)
    moved_queries = query_part - jnp.dot(solved[:, :block_size].T, vectors, precision=highest)
    moved_keys = key_part - jnp.dot(solved[:, block_size:2 * block_size].T, vectors, precision=highest)
    product = jnp.eye(feature_width, dtype=jnp.float32) - jnp.dot(vectors.T, solved[:, 2 * block_size:], precision=highest)
    return (moved_queries, moved_keys, product)

def reference(queries, key_rows, value_rows, reflections, segment_ids, head_gains):
    score_scale = 1.0 / math.sqrt(HD)
    blocks = LENGTH // BLK
    positions = jnp.arange(LENGTH, dtype=jnp.int32)
    causal = positions[:, None] >= positions[None, :]
    identity = jnp.eye(HD, dtype=jnp.float32)

    def one_head(operands):
        query_part, key_part, value_part, raw_rows, gain_part, segments = operands
        vectors = normalized(raw_rows).reshape(blocks, BLK, HD)
        moved_q, moved_k, products = jax.vmap(block_terms)(vectors, query_part.astype(jnp.float32).reshape(blocks, BLK, HD), key_part.astype(jnp.float32).reshape(blocks, BLK, HD))

        def chain_step(running, product):
            return (jnp.dot(running, product, precision=highest), running)
        remaining, before = lax.scan(chain_step, identity, products)
        rotated_q = jnp.einsum('btd,bed->bte', moved_q, before, precision=highest).reshape(LENGTH, HD).astype(jnp.bfloat16)
        rotated_k = jnp.einsum('btd,bed->bte', moved_k, before, precision=highest).reshape(LENGTH, HD).astype(jnp.bfloat16)
        scores = jnp.dot(rotated_q, rotated_k.T, preferred_element_type=jnp.float32) * score_scale
        allowed = causal & (segments[:, None] == segments[None, :])
        masked = jnp.where(allowed, scores, neg_large)
        probable = jnp.where(allowed, jnp.exp(masked - lax.optimization_barrier(jnp.max(masked, axis=-1, keepdims=True))), 0.0)
        mixed = jnp.dot(probable.astype(jnp.bfloat16), value_part, preferred_element_type=jnp.float32)
        mixed = mixed / lax.optimization_barrier(jnp.sum(probable, axis=-1, keepdims=True))
        return mixed * gain_part[None, :]

    def one_sequence(operands):
        query_seq, key_seq, value_seq, raw_seq, segments = operands

        def heads_major(array):
            return array.reshape(LENGTH, HEADS, HD).transpose(1, 0, 2)
        gain_heads = head_gains.reshape(HEADS, HD)
        segment_copies = jnp.broadcast_to(segments, (HEADS, LENGTH))
        per_head = lax.map(one_head, (heads_major(query_seq), heads_major(key_seq), heads_major(value_seq), heads_major(raw_seq), gain_heads, segment_copies))
        return per_head.transpose(1, 0, 2).reshape(LENGTH, HEADS * HD).astype(jnp.bfloat16)
    return lax.map(one_sequence, (queries, key_rows, value_rows, reflections, segment_ids))
```

```python
import functools
import math

import jax
import jax.numpy as jnp
from jax import lax
from jax.experimental import pallas as pl
from jax.experimental.pallas import tpu as pltpu
from jax.sharding import PartitionSpec as P

HEADS = 16
HD = 128
TOK = 128
LENGTH = 2048
BAND = 1024
ROWS = 256
SPAN = BAND + ROWS
BLOCKS = LENGTH // TOK
GROUP = 4
EPSILON = 1e-06
FAR = 2.0**100
F32 = jnp.float32
BF16 = jnp.bfloat16
MESH = pl.DeviceIdType.MESH


def dot(a, b):
    return lax.dot_general(a, b, (((1,), (0,)), ((), ())), preferred_element_type=F32)


def dot_nt(a, b):
    return lax.dot_general(a, b, (((1,), (1,)), ((), ())), preferred_element_type=F32)


def dot_tn(a, b):
    return lax.dot_general(a, b, (((0,), (0,)), ((), ())), preferred_element_type=F32)


def halves(x):
    high = x.astype(BF16)
    return high, (x - high.astype(F32)).astype(BF16)


def beside(a, b):
    return jnp.concatenate([a, b], axis=1)


def below(a, b):
    return jnp.concatenate([a, b], axis=0)


def product(a_high, a_low, b_high, b_low):
    return dot(beside(a_high, a_low), below(b_high, b_high)) + dot(a_high, b_low)


def at_block(index, size=TOK):
    return pl.ds(pl.multiple_of(index * size, size), size)


def square_iota():
    i = lax.broadcasted_iota(jnp.int32, (TOK, TOK), 0)
    j = lax.broadcasted_iota(jnp.int32, (TOK, TOK), 1)
    return i, j


def merge_reflections(r_buf, y_buf):
    i, j = square_iota()
    apart = jnp.bitwise_xor(i, j)

    def group(g, carry):
        raws, merged, betas = [], [], []
        for u in range(GROUP):
            raw = r_buf[at_block(g * GROUP + u), :]
            wide = raw.astype(F32)
            beta = 2.0 / (jnp.sum(wide * wide, axis=1, keepdims=True) + EPSILON)
            raws.append(raw)
            betas.append(beta)
            merged.append(wide * beta)
        for level in range(7):
            chosen = (lax.shift_right_logical(apart, level) == 1) & (i > j)
            for u in range(GROUP):
                raw = raws[u]
                high, low = halves(merged[u])
                if level == 0:
                    cross = dot_nt(raw, raw) * betas[u]
                else:
                    cross = dot_nt(beside(high, low), beside(raw, raw))
                c_high, c_low = halves(jnp.where(chosen, cross, 0.0))
                merged[u] = merged[u] - product(c_high, c_low, high, low)
        for u in range(GROUP):
            y_buf[at_block(g * GROUP + u), :] = merged[u]
        return carry

    lax.fori_loop(0, BLOCKS // GROUP, group, 0)


def chain_blocks(r_buf, y_buf, w_buf):
    i, j = square_iota()

    def step(b, before):
        raw = r_buf[at_block(b), :]
        a_high, a_low = halves(before)
        y_high, y_low = halves(y_buf[at_block(b), :])
        z_high, z_low = halves(product(y_high, y_low, a_high, a_low))
        w_buf[b, :TOK, :TOK] = a_high
        w_buf[b, :TOK, TOK:] = a_low
        w_buf[b, TOK:, :TOK] = -z_high
        w_buf[b, TOK:, TOK:] = -z_low
        return before - dot_tn(below(raw, raw), below(z_high, z_low))

    lax.fori_loop(0, BLOCKS, step, jnp.where(i == j, 1.0, 0.0).astype(F32))


def rotate(x_buf, r_buf, w_buf, put):
    i, j = square_iota()

    def some(g, carry):
        for u in range(GROUP):
            b = g * GROUP + u
            raw_x = x_buf[at_block(b), :]
            seen = jnp.where(i >= j, dot_nt(raw_x, r_buf[at_block(b), :]), 0.0)
            s_high, s_low = halves(seen)
            both = dot(beside(raw_x, s_high), w_buf[b])
            rest = dot(s_low, w_buf[b, TOK:, :TOK])
            put(b, (both[:, :TOK] + both[:, TOK:] + rest).astype(BF16))
        return carry

    lax.fori_loop(0, BLOCKS // GROUP, some, 0)


def place_documents(segments, q_full, k_full):
    i, _ = square_iota()

    def one(b, carry):
        hot = jnp.where(segments[b] == i, 1.0, 0.0).astype(F32).T
        q_full[at_block(b), TOK:] = (hot * FAR).astype(BF16)
        k_full[pl.ds(pl.multiple_of(BAND + b * TOK, TOK), TOK), TOK:] = (hot - 1.0).astype(BF16)
        return carry

    lax.fori_loop(0, BLOCKS, one, 0)


def prepare_bands(k_full, v_full):
    k_full[:BAND, :TOK] = jnp.zeros((BAND, TOK), BF16)
    k_full[:BAND, TOK:] = jnp.full((BAND, TOK), -1.0, BF16)
    v_full[:BAND, :TOK] = jnp.zeros((BAND, TOK), BF16)
    v_full[:, TOK:] = jnp.ones((BAND + LENGTH, TOK), BF16)


def weigh(q_full, k_full, s_buf, p_buf):
    i = lax.broadcasted_iota(jnp.int32, (ROWS, ROWS), 0)
    j = lax.broadcasted_iota(jnp.int32, (ROWS, ROWS), 1)
    scale = math.log2(math.e) / math.sqrt(HD)

    def tile(t, carry):
        q_rows = q_full[at_block(t, ROWS), :]
        most = None
        for n in range(SPAN // ROWS):
            keys = k_full[pl.ds(pl.multiple_of((t + n) * ROWS, ROWS), ROWS), :]
            scores = dot_nt(q_rows, keys)
            if n == SPAN // ROWS - 1:
                scores = jnp.where(i >= j, scores, -FAR)
            s_buf[:, n * ROWS : (n + 1) * ROWS] = scores
            folded = jnp.maximum(scores[:, :TOK], scores[:, TOK:])
            most = folded if most is None else jnp.maximum(most, folded)
        top = jnp.max(most, axis=1, keepdims=True)
        for n in range(SPAN // ROWS):
            piece = slice(n * ROWS, (n + 1) * ROWS)
            p_buf[t, :, piece] = jnp.exp2((s_buf[:, piece] - top) * scale).astype(BF16)
        return carry

    lax.fori_loop(0, LENGTH // ROWS, tile, 0)


def mix(t, p_buf, v_full, gains, o_buf):
    both = dot(p_buf[t], v_full[pl.ds(pl.multiple_of(t * ROWS, ROWS), SPAN), :])
    o_buf[at_block(t, ROWS), :] = (both[:, :TOK] / both[:, TOK:] * gains[...]).astype(BF16)


def kernel(
    q_in, k_in, v_in, r_in, segment_in, gain_in, out,
    r_buf, q_buf, k_buf, v_full, segments, gains,
    y_buf, w_buf, q_full, k_full, s_buf, p_buf, o_buf,
    send_sem, recv_sem, own_sem, out_send, out_recv, out_own, gain_send, gain_recv, gain_own,
):
    row, me = lax.axis_index("dp"), lax.axis_index("ctx")
    count = BLOCKS
    crossed = {"dp": me, "ctx": row}
    away = row != me

    def partner(d):
        return lax.rem(me + d, count)

    def source(a, t):
        if a == 4:
            return segment_in
        return (r_in, q_in, k_in, v_in)[a].at[0, :, at_block(t)]

    def target(a):
        if a == 4:
            return segments.at[me]
        if a == 3:
            return v_full.at[pl.ds(pl.multiple_of(BAND + me * TOK, TOK), TOK), pl.ds(0, TOK)]
        return (r_buf, q_buf, k_buf)[a].at[at_block(me), :]

    def remote(a, d):
        t = partner(d)
        return pltpu.make_async_remote_copy(
            src_ref=source(a, t), dst_ref=target(a), send_sem=send_sem.at[a, d], recv_sem=recv_sem.at[a, d],
            device_id={"ctx": t}, device_id_type=MESH,
        )

    def own(a):
        return pltpu.make_async_copy(source(a, me), target(a), own_sem.at[a])

    def gain_copy():
        return pltpu.make_async_remote_copy(
            src_ref=gain_in, dst_ref=gains, send_sem=gain_send, recv_sem=gain_recv,
            device_id=crossed, device_id_type=MESH,
        )

    def each_partner(act):
        def one(d, carry):
            act(d)
            return carry

        lax.fori_loop(1, count, one, 0)

    def arrive(a):
        own(a).wait()
        each_partner(lambda d: remote(a, d).wait_recv())

    for a in range(5):
        own(a).start()
    barrier = pltpu.get_barrier_semaphore()
    each_partner(
        lambda d: pl.semaphore_signal(barrier, inc=1, device_id={"ctx": partner(d)}, device_id_type=MESH)
    )

    @pl.when(away)
    def _():
        pl.semaphore_signal(barrier, inc=1, device_id=crossed, device_id_type=MESH)

    pl.semaphore_wait(barrier, jnp.where(away, count, count - 1))

    for a in (0, 4, 1, 2, 3):
        each_partner(lambda d, a=a: remote(a, d).start())

    @pl.when(away)
    def _():
        gain_copy().start()

    @pl.when(jnp.logical_not(away))
    def _():
        pltpu.make_async_copy(gain_in, gains, gain_own).start()

    prepare_bands(k_full, v_full)
    arrive(0)
    merge_reflections(r_buf, y_buf)
    chain_blocks(r_buf, y_buf, w_buf)
    arrive(4)
    place_documents(segments, q_full, k_full)
    arrive(1)

    def put_query(b, rows):
        q_full[at_block(b), :TOK] = rows

    def put_key(b, rows):
        k_full[pl.ds(pl.multiple_of(BAND + b * TOK, TOK), TOK), :TOK] = rows

    rotate(q_buf, r_buf, w_buf, put_query)
    arrive(2)
    rotate(k_buf, r_buf, w_buf, put_key)
    weigh(q_full, k_full, s_buf, p_buf)

    @pl.when(away)
    def _():
        gain_copy().wait()

    @pl.when(jnp.logical_not(away))
    def _():
        pltpu.make_async_copy(gain_in, gains, gain_own).wait()

    arrive(3)

    def out_copy(t):
        return pltpu.make_async_remote_copy(
            src_ref=o_buf.at[at_block(t), :], dst_ref=out.at[0, :, at_block(me)],
            send_sem=out_send.at[t], recv_sem=out_recv.at[me], device_id={"ctx": t}, device_id_type=MESH,
        )

    def out_own_copy():
        return pltpu.make_async_copy(o_buf.at[at_block(me), :], out.at[0, :, at_block(me)], out_own)

    def finish(n, carry):
        tile = lax.rem(me // 2 + n, LENGTH // ROWS)
        mix(tile, p_buf, v_full, gains, o_buf)
        for half in range(ROWS // TOK):
            t = tile * (ROWS // TOK) + half

            @pl.when(t != me)
            def _():
                out_copy(t).start()

            @pl.when(t == me)
            def _():
                out_own_copy().start()

        return carry

    lax.fori_loop(0, LENGTH // ROWS, finish, 0)

    for a in range(5):
        each_partner(lambda d, a=a: remote(a, d).wait_send())
    each_partner(lambda d: out_copy(partner(d)).wait_send())

    def out_arrived(d):
        s = partner(d)
        pltpu.make_async_remote_copy(
            src_ref=o_buf.at[at_block(s), :], dst_ref=out.at[0, :, at_block(s)],
            send_sem=out_send.at[s], recv_sem=out_recv.at[s], device_id={"ctx": s}, device_id_type=MESH,
        ).wait_recv()

    each_partner(out_arrived)
    out_own_copy().wait()


def local(queries, key_rows, value_rows, reflections, segment_ids, head_gains):
    hbm = pl.BlockSpec(memory_space=pltpu.HBM)
    vmem = pl.BlockSpec(memory_space=pltpu.VMEM)
    dma = pltpu.SemaphoreType.DMA
    return pl.pallas_call(
        kernel,
        out_shape=jax.ShapeDtypeStruct((1, TOK, HEADS * HD), BF16),
        in_specs=[hbm, hbm, hbm, hbm, vmem, vmem],
        out_specs=hbm,
        scratch_shapes=[
            pltpu.VMEM((LENGTH, HD), BF16),
            pltpu.VMEM((LENGTH, HD), BF16),
            pltpu.VMEM((LENGTH, HD), BF16),
            pltpu.VMEM((BAND + LENGTH, 2 * HD), BF16),
            pltpu.VMEM((BLOCKS, 1, TOK), jnp.int32),
            pltpu.VMEM((1, HD), F32),
            pltpu.VMEM((LENGTH, HD), F32),
            pltpu.VMEM((BLOCKS, 2 * HD, 2 * HD), BF16),
            pltpu.VMEM((LENGTH, 2 * HD), BF16),
            pltpu.VMEM((BAND + LENGTH, 2 * HD), BF16),
            pltpu.VMEM((ROWS, SPAN), F32),
            pltpu.VMEM((LENGTH // ROWS, ROWS, SPAN), BF16),
            pltpu.VMEM((LENGTH, HD), BF16),
            dma((5, BLOCKS)),
            dma((5, BLOCKS)),
            dma((5,)),
            dma((BLOCKS,)),
            dma((BLOCKS,)),
            dma,
            dma,
            dma,
            dma,
        ],
        compiler_params=pltpu.CompilerParams(
            collective_id=0, has_side_effects=True, vmem_limit_bytes=63 * 1024 * 1024
        ),
    )(queries, key_rows, value_rows, reflections, segment_ids, head_gains[None, :])


def solution(mesh):
    placed = (
        P("dp", "ctx", None),
        P("dp", "ctx", None),
        P("dp", "ctx", None),
        P("dp", "ctx", None),
        P("dp", "ctx"),
        P("dp"),
    )
    return jax.shard_map(
        local, mesh=mesh, in_specs=placed, out_specs=P("dp", "ctx", None), check_vma=False
    )
```

```python
import functools
import math

import jax
import jax.numpy as jnp
from jax import lax
from jax.experimental import pallas as pl
from jax.experimental.pallas import tpu as pltpu
from jax.sharding import PartitionSpec as P

HEADS = 16
HD = 128
TOK = 128
LENGTH = 2048
BAND = 1024
ROWS = 256
SPAN = BAND + ROWS
BLOCKS = LENGTH // TOK
GROUP = 4
EPSILON = 1e-06
FAR = 2.0**100
F32 = jnp.float32
BF16 = jnp.bfloat16
MESH = pl.DeviceIdType.MESH


def dot(a, b):
    return lax.dot_general(a, b, (((1,), (0,)), ((), ())), preferred_element_type=F32)


def dot_nt(a, b):
    return lax.dot_general(a, b, (((1,), (1,)), ((), ())), preferred_element_type=F32)


def dot_tn(a, b):
    return lax.dot_general(a, b, (((0,), (0,)), ((), ())), preferred_element_type=F32)


def halves(x):
    high = x.astype(BF16)
    return high, (x - high.astype(F32)).astype(BF16)


def beside(a, b):
    return jnp.concatenate([a, b], axis=1)


def below(a, b):
    return jnp.concatenate([a, b], axis=0)


def product(a_high, a_low, b_high, b_low):
    return dot(beside(a_high, a_low), below(b_high, b_high)) + dot(a_high, b_low)


def at_block(index, size=TOK):
    return pl.ds(pl.multiple_of(index * size, size), size)


def square_iota():
    i = lax.broadcasted_iota(jnp.int32, (TOK, TOK), 0)
    j = lax.broadcasted_iota(jnp.int32, (TOK, TOK), 1)
    return i, j


def merge_reflections(r_buf, y_buf):
    i, j = square_iota()
    apart = jnp.bitwise_xor(i, j)

    def group(g, carry):
        raws, merged, betas = [], [], []
        for u in range(GROUP):
            raw = r_buf[at_block(g * GROUP + u), :]
            wide = raw.astype(F32)
            beta = 2.0 / (jnp.sum(wide * wide, axis=1, keepdims=True) + EPSILON)
            raws.append(raw)
            betas.append(beta)
            merged.append(wide * beta)
        for level in range(7):
            chosen = (lax.shift_right_logical(apart, level) == 1) & (i > j)
            for u in range(GROUP):
                raw = raws[u]
                high, low = halves(merged[u])
                if level == 0:
                    cross = dot_nt(raw, raw) * betas[u]
                else:
                    cross = dot_nt(beside(high, low), beside(raw, raw))
                c_high, c_low = halves(jnp.where(chosen, cross, 0.0))
                merged[u] = merged[u] - product(c_high, c_low, high, low)
        for u in range(GROUP):
            y_buf[at_block(g * GROUP + u), :] = merged[u]
        return carry

    lax.fori_loop(0, BLOCKS // GROUP, group, 0)


def chain_blocks(r_buf, y_buf, w_buf):
    i, j = square_iota()

    def step(b, before):
        raw = r_buf[at_block(b), :]
        a_high, a_low = halves(before)
        y_high, y_low = halves(y_buf[at_block(b), :])
        z_high, z_low = halves(product(y_high, y_low, a_high, a_low))
        w_buf[b, :TOK, :TOK] = a_high
        w_buf[b, :TOK, TOK:] = a_low
        w_buf[b, TOK:, :TOK] = -z_high
        w_buf[b, TOK:, TOK:] = -z_low
        return before - dot_tn(below(raw, raw), below(z_high, z_low))

    lax.fori_loop(0, BLOCKS, step, jnp.where(i == j, 1.0, 0.0).astype(F32))


def rotate(x_buf, r_buf, w_buf, put):
    i, j = square_iota()

    def some(g, carry):
        for u in range(GROUP):
            b = g * GROUP + u
            raw_x = x_buf[at_block(b), :]
            seen = jnp.where(i >= j, dot_nt(raw_x, r_buf[at_block(b), :]), 0.0)
            s_high, s_low = halves(seen)
            both = dot(beside(raw_x, s_high), w_buf[b])
            rest = dot(s_low, w_buf[b, TOK:, :TOK])
            put(b, (both[:, :TOK] + both[:, TOK:] + rest).astype(BF16))
        return carry

    lax.fori_loop(0, BLOCKS // GROUP, some, 0)


def place_documents(segments, q_full, k_full):
    i, _ = square_iota()

    def one(b, carry):
        hot = jnp.where(segments[b] == i, 1.0, 0.0).astype(F32).T
        q_full[at_block(b), TOK:] = (hot * FAR).astype(BF16)
        k_full[pl.ds(pl.multiple_of(BAND + b * TOK, TOK), TOK), TOK:] = (hot - 1.0).astype(BF16)
        return carry

    lax.fori_loop(0, BLOCKS, one, 0)


def prepare_bands(k_full, v_full):
    k_full[:BAND, :TOK] = jnp.zeros((BAND, TOK), BF16)
    k_full[:BAND, TOK:] = jnp.full((BAND, TOK), -1.0, BF16)
    v_full[:BAND, :TOK] = jnp.zeros((BAND, TOK), BF16)
    v_full[:, TOK:] = jnp.ones((BAND + LENGTH, TOK), BF16)


def weigh(q_full, k_full, s_buf, p_buf):
    i = lax.broadcasted_iota(jnp.int32, (ROWS, ROWS), 0)
    j = lax.broadcasted_iota(jnp.int32, (ROWS, ROWS), 1)
    scale = math.log2(math.e) / math.sqrt(HD)

    def tile(t, carry):
        q_rows = q_full[at_block(t, ROWS), :]
        most = None
        for n in range(SPAN // ROWS):
            keys = k_full[pl.ds(pl.multiple_of((t + n) * ROWS, ROWS), ROWS), :]
            scores = dot_nt(q_rows, keys)
            if n == SPAN // ROWS - 1:
                scores = jnp.where(i >= j, scores, -FAR)
            s_buf[:, n * ROWS : (n + 1) * ROWS] = scores
            folded = jnp.maximum(scores[:, :TOK], scores[:, TOK:])
            most = folded if most is None else jnp.maximum(most, folded)
        top = jnp.max(most, axis=1, keepdims=True)
        for n in range(SPAN // ROWS):
            piece = slice(n * ROWS, (n + 1) * ROWS)
            p_buf[t, :, piece] = jnp.exp2((s_buf[:, piece] - top) * scale).astype(BF16)
        return carry

    lax.fori_loop(0, LENGTH // ROWS, tile, 0)


def mix(t, p_buf, v_full, gains, o_buf):
    both = dot(p_buf[t], v_full[pl.ds(pl.multiple_of(t * ROWS, ROWS), SPAN), :])
    o_buf[at_block(t, ROWS), :] = (both[:, :TOK] / both[:, TOK:] * gains[...]).astype(BF16)


def kernel(
    q_in, k_in, v_in, r_in, segment_in, gain_in, out,
    r_buf, q_buf, k_buf, v_full, segments, gains,
    y_buf, w_buf, q_full, k_full, s_buf, p_buf, o_buf,
    send_sem, recv_sem, own_sem, out_send, out_recv, out_own, gain_send, gain_recv, gain_own,
):
    row, me = lax.axis_index("dp"), lax.axis_index("ctx")
    count = BLOCKS
    crossed = {"dp": me, "ctx": row}
    away = row != me

    def partner(d):
        return lax.rem(me + d, count)

    def source(a, t):
        if a == 4:
            return segment_in
        return (r_in, q_in, k_in, v_in)[a].at[0, :, at_block(t)]

    def target(a):
        if a == 4:
            return segments.at[me]
        if a == 3:
            return v_full.at[pl.ds(pl.multiple_of(BAND + me * TOK, TOK), TOK), pl.ds(0, TOK)]
        return (r_buf, q_buf, k_buf)[a].at[at_block(me), :]

    def remote(a, d):
        t = partner(d)
        return pltpu.make_async_remote_copy(
            src_ref=source(a, t), dst_ref=target(a), send_sem=send_sem.at[a, d], recv_sem=recv_sem.at[a, d],
            device_id={"ctx": t}, device_id_type=MESH,
        )

    def own(a):
        return pltpu.make_async_copy(source(a, me), target(a), own_sem.at[a])

    def gain_copy():
        return pltpu.make_async_remote_copy(
            src_ref=gain_in, dst_ref=gains, send_sem=gain_send, recv_sem=gain_recv,
            device_id=crossed, device_id_type=MESH,
        )

    def each_partner(act):
        def one(d, carry):
            act(d)
            return carry

        lax.fori_loop(1, count, one, 0)

    def arrive(a):
        own(a).wait()
        each_partner(lambda d: remote(a, d).wait_recv())

    for a in range(5):
        own(a).start()
    barrier = pltpu.get_barrier_semaphore()
    each_partner(
        lambda d: pl.semaphore_signal(barrier, inc=1, device_id={"ctx": partner(d)}, device_id_type=MESH)
    )

    @pl.when(away)
    def _():
        pl.semaphore_signal(barrier, inc=1, device_id=crossed, device_id_type=MESH)

    pl.semaphore_wait(barrier, jnp.where(away, count, count - 1))

    @pl.when(away)
    def _():
        gain_copy().start()

    @pl.when(jnp.logical_not(away))
    def _():
        pltpu.make_async_copy(gain_in, gains, gain_own).start()

    for a in (4, 0, 1, 2, 3):
        each_partner(lambda d, a=a: remote(a, d).start())

    prepare_bands(k_full, v_full)
    arrive(0)
    merge_reflections(r_buf, y_buf)
    chain_blocks(r_buf, y_buf, w_buf)
    arrive(4)
    place_documents(segments, q_full, k_full)
    arrive(1)

    def put_query(b, rows):
        q_full[at_block(b), :TOK] = rows

    def put_key(b, rows):
        k_full[pl.ds(pl.multiple_of(BAND + b * TOK, TOK), TOK), :TOK] = rows

    rotate(q_buf, r_buf, w_buf, put_query)
    arrive(2)
    rotate(k_buf, r_buf, w_buf, put_key)
    weigh(q_full, k_full, s_buf, p_buf)

    @pl.when(away)
    def _():
        gain_copy().wait()

    @pl.when(jnp.logical_not(away))
    def _():
        pltpu.make_async_copy(gain_in, gains, gain_own).wait()

    arrive(3)

    def out_copy(t):
        return pltpu.make_async_remote_copy(
            src_ref=o_buf.at[at_block(t), :], dst_ref=out.at[0, :, at_block(me)],
            send_sem=out_send.at[t], recv_sem=out_recv.at[me], device_id={"ctx": t}, device_id_type=MESH,
        )

    def out_own_copy():
        return pltpu.make_async_copy(o_buf.at[at_block(me), :], out.at[0, :, at_block(me)], out_own)

    def finish(n, carry):
        tile = lax.rem(me // 2 + n + 1, LENGTH // ROWS)
        mix(tile, p_buf, v_full, gains, o_buf)
        for half in range(ROWS // TOK):
            t = tile * (ROWS // TOK) + half

            @pl.when(t != me)
            def _():
                out_copy(t).start()

            @pl.when(t == me)
            def _():
                out_own_copy().start()

        return carry

    lax.fori_loop(0, LENGTH // ROWS, finish, 0)

    for a in range(5):
        each_partner(lambda d, a=a: remote(a, d).wait_send())
    each_partner(lambda d: out_copy(partner(d)).wait_send())

    def out_arrived(d):
        s = partner(d)
        pltpu.make_async_remote_copy(
            src_ref=o_buf.at[at_block(s), :], dst_ref=out.at[0, :, at_block(s)],
            send_sem=out_send.at[s], recv_sem=out_recv.at[s], device_id={"ctx": s}, device_id_type=MESH,
        ).wait_recv()

    each_partner(out_arrived)
    out_own_copy().wait()


def local(queries, key_rows, value_rows, reflections, segment_ids, head_gains):
    hbm = pl.BlockSpec(memory_space=pltpu.HBM)
    vmem = pl.BlockSpec(memory_space=pltpu.VMEM)
    dma = pltpu.SemaphoreType.DMA
    return pl.pallas_call(
        kernel,
        out_shape=pltpu.VMEM((1, TOK, HEADS * HD), BF16),
        in_specs=[hbm, hbm, hbm, hbm, vmem, vmem],
        out_specs=pl.BlockSpec(memory_space=pl.ANY),
        scratch_shapes=[
            pltpu.VMEM((LENGTH, HD), BF16),
            pltpu.VMEM((LENGTH, HD), BF16),
            pltpu.VMEM((LENGTH, HD), BF16),
            pltpu.VMEM((BAND + LENGTH, 2 * HD), BF16),
            pltpu.VMEM((BLOCKS, 1, TOK), jnp.int32),
            pltpu.VMEM((1, HD), F32),
            pltpu.VMEM((LENGTH, HD), F32),
            pltpu.VMEM((BLOCKS, 2 * HD, 2 * HD), BF16),
            pltpu.VMEM((LENGTH, 2 * HD), BF16),
            pltpu.VMEM((BAND + LENGTH, 2 * HD), BF16),
            pltpu.VMEM((ROWS, SPAN), F32),
            pltpu.VMEM((LENGTH // ROWS, ROWS, SPAN), BF16),
            pltpu.VMEM((LENGTH, HD), BF16),
            dma((5, BLOCKS)),
            dma((5, BLOCKS)),
            dma((5,)),
            dma((BLOCKS,)),
            dma((BLOCKS,)),
            dma,
            dma,
            dma,
            dma,
        ],
        compiler_params=pltpu.CompilerParams(
            collective_id=0, has_side_effects=True, vmem_limit_bytes=63 * 1024 * 1024
        ),
    )(queries, key_rows, value_rows, reflections, segment_ids, head_gains[None, :])


def solution(mesh):
    placed = (
        P("dp", "ctx", None),
        P("dp", "ctx", None),
        P("dp", "ctx", None),
        P("dp", "ctx", None),
        P("dp", "ctx"),
        P("dp"),
    )
    return jax.shard_map(
        local, mesh=mesh, in_specs=placed, out_specs=P("dp", "ctx", None), check_vma=False
    )
```

```python
import functools
import math

import jax
import jax.numpy as jnp
from jax import lax
from jax.experimental import pallas as pl
from jax.experimental.pallas import tpu as pltpu
from jax.sharding import PartitionSpec as P

HEADS = 16
HD = 128
TOK = 128
LENGTH = 2048
BAND = 1024
ROWS = 256
SPAN = BAND + ROWS
BLOCKS = LENGTH // TOK
GROUP = 4
EPSILON = 1e-06
FAR = 2.0**100
F32 = jnp.float32
BF16 = jnp.bfloat16
MESH = pl.DeviceIdType.MESH


def dot(a, b):
    return lax.dot_general(a, b, (((1,), (0,)), ((), ())), preferred_element_type=F32)


def dot_nt(a, b):
    return lax.dot_general(a, b, (((1,), (1,)), ((), ())), preferred_element_type=F32)


def dot_tn(a, b):
    return lax.dot_general(a, b, (((0,), (0,)), ((), ())), preferred_element_type=F32)


def halves(x):
    high = x.astype(BF16)
    return high, (x - high.astype(F32)).astype(BF16)


def beside(a, b):
    return jnp.concatenate([a, b], axis=1)


def below(a, b):
    return jnp.concatenate([a, b], axis=0)


def product(a_high, a_low, b_high, b_low):
    return dot(beside(a_high, a_low), below(b_high, b_high)) + dot(a_high, b_low)


def at_block(index, size=TOK):
    return pl.ds(pl.multiple_of(index * size, size), size)


def square_iota():
    i = lax.broadcasted_iota(jnp.int32, (TOK, TOK), 0)
    j = lax.broadcasted_iota(jnp.int32, (TOK, TOK), 1)
    return i, j


def merge_reflections(r_buf, y_buf):
    i, j = square_iota()
    apart = jnp.bitwise_xor(i, j)

    def group(g, carry):
        raws, merged, betas = [], [], []
        for u in range(GROUP):
            raw = r_buf[at_block(g * GROUP + u), :]
            wide = raw.astype(F32)
            beta = 2.0 / (jnp.sum(wide * wide, axis=1, keepdims=True) + EPSILON)
            raws.append(raw)
            betas.append(beta)
            merged.append(wide * beta)
        for level in range(7):
            chosen = (lax.shift_right_logical(apart, level) == 1) & (i > j)
            for u in range(GROUP):
                raw = raws[u]
                high, low = halves(merged[u])
                if level == 0:
                    cross = dot_nt(raw, raw) * betas[u]
                else:
                    cross = dot_nt(beside(high, low), beside(raw, raw))
                c_high, c_low = halves(jnp.where(chosen, cross, 0.0))
                merged[u] = merged[u] - product(c_high, c_low, high, low)
        for u in range(GROUP):
            y_buf[at_block(g * GROUP + u), :] = merged[u]
        return carry

    lax.fori_loop(0, BLOCKS // GROUP, group, 0)


def chain_blocks(r_buf, y_buf, w_buf):
    i, j = square_iota()

    def step(b, before):
        raw = r_buf[at_block(b), :]
        a_high, a_low = halves(before)
        y_high, y_low = halves(y_buf[at_block(b), :])
        z_high, z_low = halves(product(y_high, y_low, a_high, a_low))
        w_buf[b, :TOK, :TOK] = a_high
        w_buf[b, :TOK, TOK:] = a_low
        w_buf[b, TOK:, :TOK] = -z_high
        w_buf[b, TOK:, TOK:] = -z_low
        return before - dot_tn(below(raw, raw), below(z_high, z_low))

    lax.fori_loop(0, BLOCKS, step, jnp.where(i == j, 1.0, 0.0).astype(F32))


def rotate(blocks, x_buf, r_buf, w_buf, put):
    i, j = square_iota()
    for b in blocks:
        raw_x = x_buf[at_block(b), :]
        seen = jnp.where(i >= j, dot_nt(raw_x, r_buf[at_block(b), :]), 0.0)
        s_high, s_low = halves(seen)
        both = dot(beside(raw_x, s_high), w_buf[b])
        rest = dot(s_low, w_buf[b, TOK:, :TOK])
        put(b, (both[:, :TOK] + both[:, TOK:] + rest).astype(BF16))


def place_documents(segments, q_full, k_full):
    i, _ = square_iota()

    def one(b, carry):
        hot = jnp.where(segments[b] == i, 1.0, 0.0).astype(F32).T
        q_full[at_block(b), TOK:] = (hot * FAR).astype(BF16)
        k_full[pl.ds(pl.multiple_of(BAND + b * TOK, TOK), TOK), TOK:] = (hot - 1.0).astype(BF16)
        return carry

    lax.fori_loop(0, BLOCKS, one, 0)


def prepare_bands(k_full, v_full):
    k_full[:BAND, :TOK] = jnp.zeros((BAND, TOK), BF16)
    k_full[:BAND, TOK:] = jnp.full((BAND, TOK), -1.0, BF16)
    v_full[:BAND, :TOK] = jnp.zeros((BAND, TOK), BF16)
    v_full[:, TOK:] = jnp.ones((BAND + LENGTH, TOK), BF16)


def weigh(t, q_full, k_full, s_buf, p_buf):
    i = lax.broadcasted_iota(jnp.int32, (ROWS, ROWS), 0)
    j = lax.broadcasted_iota(jnp.int32, (ROWS, ROWS), 1)
    scale = math.log2(math.e) / math.sqrt(HD)
    q_rows = q_full[at_block(t, ROWS), :]
    most = None
    for n in range(SPAN // ROWS):
        keys = k_full[pl.ds(pl.multiple_of((t + n) * ROWS, ROWS), ROWS), :]
        scores = dot_nt(q_rows, keys)
        if n == SPAN // ROWS - 1:
            scores = jnp.where(i >= j, scores, -FAR)
        s_buf[:, n * ROWS : (n + 1) * ROWS] = scores
        folded = jnp.maximum(scores[:, :TOK], scores[:, TOK:])
        most = folded if most is None else jnp.maximum(most, folded)
    top = jnp.max(most, axis=1, keepdims=True)
    for n in range(SPAN // ROWS):
        piece = slice(n * ROWS, (n + 1) * ROWS)
        p_buf[:, piece] = jnp.exp2((s_buf[:, piece] - top) * scale).astype(BF16)


def mix(t, p_buf, v_full, gains, o_buf):
    both = dot(p_buf[...], v_full[pl.ds(pl.multiple_of(t * ROWS, ROWS), SPAN), :])
    o_buf[at_block(t, ROWS), :] = (both[:, :TOK] / both[:, TOK:] * gains[...]).astype(BF16)


def kernel(
    q_in, k_in, v_in, r_in, segment_in, gain_in, out,
    r_buf, q_buf, k_buf, v_full, segments, gains,
    y_buf, w_buf, q_full, k_full, s_buf, p_buf, o_buf,
    send_sem, recv_sem, own_sem, out_send, out_recv, out_own, gain_send, gain_recv, gain_own,
):
    row, me = lax.axis_index("dp"), lax.axis_index("ctx")
    count = BLOCKS
    crossed = {"dp": me, "ctx": row}
    away = row != me

    tiles = LENGTH // ROWS
    pair, half = me // 2, lax.rem(me, 2)

    def partner(d):
        return 2 * lax.rem(pair + d // 2, tiles) + lax.rem(half + d, 2)

    def source(a, t):
        if a == 4:
            return segment_in
        return (r_in, q_in, k_in, v_in)[a].at[0, :, at_block(t)]

    def target(a):
        if a == 4:
            return segments.at[me]
        if a == 3:
            return v_full.at[pl.ds(pl.multiple_of(BAND + me * TOK, TOK), TOK), pl.ds(0, TOK)]
        return (r_buf, q_buf, k_buf)[a].at[at_block(me), :]

    def remote(a, d):
        t = partner(d)
        return pltpu.make_async_remote_copy(
            src_ref=source(a, t), dst_ref=target(a), send_sem=send_sem.at[a, d], recv_sem=recv_sem.at[a, d],
            device_id={"ctx": t}, device_id_type=MESH,
        )

    def own(a):
        return pltpu.make_async_copy(source(a, me), target(a), own_sem.at[a])

    def gain_copy():
        return pltpu.make_async_remote_copy(
            src_ref=gain_in, dst_ref=gains, send_sem=gain_send, recv_sem=gain_recv,
            device_id=crossed, device_id_type=MESH,
        )

    def each_partner(act):
        def one(d, carry):
            act(d)
            return carry

        lax.fori_loop(1, count, one, 0)

    def arrive(a):
        own(a).wait()
        each_partner(lambda d: remote(a, d).wait_recv())

    for a in range(5):
        own(a).start()
    barrier = pltpu.get_barrier_semaphore()
    each_partner(
        lambda d: pl.semaphore_signal(barrier, inc=1, device_id={"ctx": partner(d)}, device_id_type=MESH)
    )

    @pl.when(away)
    def _():
        pl.semaphore_signal(barrier, inc=1, device_id=crossed, device_id_type=MESH)

    pl.semaphore_wait(barrier, jnp.where(away, count, count - 1))

    @pl.when(away)
    def _():
        gain_copy().start()

    @pl.when(jnp.logical_not(away))
    def _():
        pltpu.make_async_copy(gain_in, gains, gain_own).start()

    for a in (4, 0, 2, 3, 1):
        each_partner(lambda d, a=a: remote(a, d).start())

    prepare_bands(k_full, v_full)
    arrive(0)
    merge_reflections(r_buf, y_buf)
    chain_blocks(r_buf, y_buf, w_buf)
    arrive(4)
    place_documents(segments, q_full, k_full)
    arrive(2)

    def put_query(b, rows):
        q_full[at_block(b), :TOK] = rows

    def put_key(b, rows):
        k_full[pl.ds(pl.multiple_of(BAND + b * TOK, TOK), TOK), :TOK] = rows

    def some_keys(g, carry):
        rotate([g * GROUP + u for u in range(GROUP)], k_buf, r_buf, w_buf, put_key)
        return carry

    lax.fori_loop(0, BLOCKS // GROUP, some_keys, 0)

    @pl.when(away)
    def _():
        gain_copy().wait()

    @pl.when(jnp.logical_not(away))
    def _():
        pltpu.make_async_copy(gain_in, gains, gain_own).wait()

    arrive(3)

    def out_copy(t):
        return pltpu.make_async_remote_copy(
            src_ref=o_buf.at[at_block(t), :], dst_ref=out.at[0, :, at_block(me)],
            send_sem=out_send.at[t], recv_sem=out_recv.at[me], device_id={"ctx": t}, device_id_type=MESH,
        )

    def out_own_copy():
        return pltpu.make_async_copy(o_buf.at[at_block(me), :], out.at[0, :, at_block(me)], out_own)

    def attend(tile):
        rotate([2 * tile, 2 * tile + 1], q_buf, r_buf, w_buf, put_query)
        weigh(tile, q_full, k_full, s_buf, p_buf)
        mix(tile, p_buf, v_full, gains, o_buf)

    own(1).wait()
    remote(1, 1).wait_recv()
    attend(pair)
    out_own_copy().start()
    out_copy(partner(1)).start()

    def finish(n, carry):
        tile = lax.rem(pair + tiles - n, tiles)
        remote(1, 2 * n).wait_recv()
        remote(1, 2 * n + 1).wait_recv()
        attend(tile)
        for h in range(2):
            out_copy(2 * tile + h).start()
        return carry

    lax.fori_loop(1, tiles, finish, 0)

    for a in range(5):
        each_partner(lambda d, a=a: remote(a, d).wait_send())
    each_partner(lambda d: out_copy(partner(d)).wait_send())

    def out_arrived(d):
        s = partner(d)
        pltpu.make_async_remote_copy(
            src_ref=o_buf.at[at_block(s), :], dst_ref=out.at[0, :, at_block(s)],
            send_sem=out_send.at[s], recv_sem=out_recv.at[s], device_id={"ctx": s}, device_id_type=MESH,
        ).wait_recv()

    each_partner(out_arrived)
    out_own_copy().wait()


def local(queries, key_rows, value_rows, reflections, segment_ids, head_gains):
    hbm = pl.BlockSpec(memory_space=pltpu.HBM)
    vmem = pl.BlockSpec(memory_space=pltpu.VMEM)
    dma = pltpu.SemaphoreType.DMA
    return pl.pallas_call(
        kernel,
        out_shape=pltpu.VMEM((1, TOK, HEADS * HD), BF16),
        in_specs=[hbm, hbm, hbm, hbm, vmem, vmem],
        out_specs=pl.BlockSpec(memory_space=pl.ANY),
        scratch_shapes=[
            pltpu.VMEM((LENGTH, HD), BF16),
            pltpu.VMEM((LENGTH, HD), BF16),
            pltpu.VMEM((LENGTH, HD), BF16),
            pltpu.VMEM((BAND + LENGTH, 2 * HD), BF16),
            pltpu.VMEM((BLOCKS, 1, TOK), jnp.int32),
            pltpu.VMEM((1, HD), F32),
            pltpu.VMEM((LENGTH, HD), F32),
            pltpu.VMEM((BLOCKS, 2 * HD, 2 * HD), BF16),
            pltpu.VMEM((LENGTH, 2 * HD), BF16),
            pltpu.VMEM((BAND + LENGTH, 2 * HD), BF16),
            pltpu.VMEM((ROWS, SPAN), F32),
            pltpu.VMEM((ROWS, SPAN), BF16),
            pltpu.VMEM((LENGTH, HD), BF16),
            dma((5, BLOCKS)),
            dma((5, BLOCKS)),
            dma((5,)),
            dma((BLOCKS,)),
            dma((BLOCKS,)),
            dma,
            dma,
            dma,
            dma,
        ],
        compiler_params=pltpu.CompilerParams(
            collective_id=0, has_side_effects=True, vmem_limit_bytes=63 * 1024 * 1024
        ),
    )(queries, key_rows, value_rows, reflections, segment_ids, head_gains[None, :])


def solution(mesh):
    placed = (
        P("dp", "ctx", None),
        P("dp", "ctx", None),
        P("dp", "ctx", None),
        P("dp", "ctx", None),
        P("dp", "ctx"),
        P("dp"),
    )
    return jax.shard_map(
        local, mesh=mesh, in_specs=placed, out_specs=P("dp", "ctx", None), check_vma=False
    )
```

```python
import functools
import math

import jax
import jax.numpy as jnp
from jax import lax
from jax.experimental import pallas as pl
from jax.experimental.pallas import tpu as pltpu
from jax.sharding import PartitionSpec as P

HEADS = 16
HD = 128
TOK = 128
LENGTH = 2048
BAND = 1024
ROWS = 256
SPAN = BAND + ROWS
BLOCKS = LENGTH // TOK
GROUP = 4
EPSILON = 1e-06
FAR = 2.0**100
F32 = jnp.float32
BF16 = jnp.bfloat16
MESH = pl.DeviceIdType.MESH


def dot(a, b):
    return lax.dot_general(a, b, (((1,), (0,)), ((), ())), preferred_element_type=F32)


def dot_nt(a, b):
    return lax.dot_general(a, b, (((1,), (1,)), ((), ())), preferred_element_type=F32)


def dot_tn(a, b):
    return lax.dot_general(a, b, (((0,), (0,)), ((), ())), preferred_element_type=F32)


def halves(x):
    high = x.astype(BF16)
    return high, (x - high.astype(F32)).astype(BF16)


def beside(a, b):
    return jnp.concatenate([a, b], axis=1)


def below(a, b):
    return jnp.concatenate([a, b], axis=0)


def product(a_high, a_low, b_high, b_low):
    return dot(beside(a_high, a_low), below(b_high, b_high)) + dot(a_high, b_low)


def at_block(index, size=TOK):
    return pl.ds(pl.multiple_of(index * size, size), size)


def square_iota():
    i = lax.broadcasted_iota(jnp.int32, (TOK, TOK), 0)
    j = lax.broadcasted_iota(jnp.int32, (TOK, TOK), 1)
    return i, j


def merge_reflections(r_buf, y_buf):
    i, j = square_iota()
    apart = jnp.bitwise_xor(i, j)

    def group(g, carry):
        raws, merged, betas = [], [], []
        for u in range(GROUP):
            raw = r_buf[at_block(g * GROUP + u), :]
            wide = raw.astype(F32)
            beta = 2.0 / (jnp.sum(wide * wide, axis=1, keepdims=True) + EPSILON)
            raws.append(raw)
            betas.append(beta)
            merged.append(wide * beta)
        for level in range(7):
            chosen = (lax.shift_right_logical(apart, level) == 1) & (i > j)
            for u in range(GROUP):
                raw = raws[u]
                high, low = halves(merged[u])
                if level == 0:
                    cross = dot_nt(raw, raw) * betas[u]
                else:
                    cross = dot_nt(beside(high, low), beside(raw, raw))
                c_high, c_low = halves(jnp.where(chosen, cross, 0.0))
                merged[u] = merged[u] - product(c_high, c_low, high, low)
        for u in range(GROUP):
            y_buf[at_block(g * GROUP + u), :] = merged[u]
        return carry

    lax.fori_loop(0, BLOCKS // GROUP, group, 0)


def chain_blocks(r_buf, y_buf, w_buf):
    i, j = square_iota()

    def step(b, before):
        raw = r_buf[at_block(b), :]
        a_high, a_low = halves(before)
        y_high, y_low = halves(y_buf[at_block(b), :])
        z_high, z_low = halves(product(y_high, y_low, a_high, a_low))
        w_buf[b, :TOK, :TOK] = a_high
        w_buf[b, :TOK, TOK:] = a_low
        w_buf[b, TOK:, :TOK] = -z_high
        w_buf[b, TOK:, TOK:] = -z_low
        return before - dot_tn(below(raw, raw), below(z_high, z_low))

    lax.fori_loop(0, BLOCKS, step, jnp.where(i == j, 1.0, 0.0).astype(F32))


def rotate(blocks, x_buf, r_buf, w_buf, put):
    i, j = square_iota()
    for b in blocks:
        raw_x = x_buf[at_block(b), :]
        seen = jnp.where(i >= j, dot_nt(raw_x, r_buf[at_block(b), :]), 0.0)
        s_high, s_low = halves(seen)
        both = dot(beside(raw_x, s_high), w_buf[b])
        rest = dot(s_low, w_buf[b, TOK:, :TOK])
        put(b, (both[:, :TOK] + both[:, TOK:] + rest).astype(BF16))


def place_documents(segments, q_full, k_full):
    i, _ = square_iota()

    def one(b, carry):
        hot = jnp.where(segments[b] == i, 1.0, 0.0).astype(F32).T
        q_full[at_block(b), TOK:] = (hot * FAR).astype(BF16)
        k_full[pl.ds(pl.multiple_of(BAND + b * TOK, TOK), TOK), TOK:] = (hot - 1.0).astype(BF16)
        return carry

    lax.fori_loop(0, BLOCKS, one, 0)


def prepare_bands(k_full, v_full):
    k_full[:BAND, :TOK] = jnp.zeros((BAND, TOK), BF16)
    k_full[:BAND, TOK:] = jnp.full((BAND, TOK), -1.0, BF16)
    v_full[:BAND, :TOK] = jnp.zeros((BAND, TOK), BF16)
    v_full[:, TOK:] = jnp.ones((BAND + LENGTH, TOK), BF16)


def weigh(t, q_full, k_full, s_buf, p_buf):
    i = lax.broadcasted_iota(jnp.int32, (ROWS, ROWS), 0)
    j = lax.broadcasted_iota(jnp.int32, (ROWS, ROWS), 1)
    scale = math.log2(math.e) / math.sqrt(HD)
    q_rows = q_full[at_block(t, ROWS), :]
    most = None
    for n in range(SPAN // ROWS):
        keys = k_full[pl.ds(pl.multiple_of((t + n) * ROWS, ROWS), ROWS), :]
        scores = dot_nt(q_rows, keys)
        if n == SPAN // ROWS - 1:
            scores = jnp.where(i >= j, scores, -FAR)
        s_buf[:, n * ROWS : (n + 1) * ROWS] = scores
        folded = jnp.maximum(scores[:, :TOK], scores[:, TOK:])
        most = folded if most is None else jnp.maximum(most, folded)
    top = jnp.max(most, axis=1, keepdims=True)
    for n in range(SPAN // ROWS):
        piece = slice(n * ROWS, (n + 1) * ROWS)
        p_buf[:, piece] = jnp.exp2((s_buf[:, piece] - top) * scale).astype(BF16)


def mix(t, p_buf, v_full, gains, o_buf):
    both = dot(p_buf[...], v_full[pl.ds(pl.multiple_of(t * ROWS, ROWS), SPAN), :])
    o_buf[at_block(t, ROWS), :] = (both[:, :TOK] / both[:, TOK:] * gains[...]).astype(BF16)


def kernel(
    q_in, k_in, v_in, r_in, segment_in, gain_in, out,
    r_buf, q_buf, k_buf, v_full, segments, gains,
    y_buf, w_buf, q_full, k_full, s_buf, p_buf, o_buf,
    send_sem, recv_sem, own_sem, q_send, q_recv, out_send, out_recv, out_own, gain_send, gain_recv, gain_own,
):
    row, me = lax.axis_index("dp"), lax.axis_index("ctx")
    count = BLOCKS
    crossed = {"dp": me, "ctx": row}
    away = row != me

    tiles = LENGTH // ROWS
    pair, half = me // 2, lax.rem(me, 2)

    def partner(d):
        return 2 * lax.rem(pair + d // 2, tiles) + lax.rem(half + d, 2)

    def source(a, t):
        if a == 3:
            return segment_in
        return (r_in, k_in, v_in)[a].at[0, :, at_block(t)]

    def target(a):
        if a == 3:
            return segments.at[me]
        if a == 2:
            return v_full.at[pl.ds(pl.multiple_of(BAND + me * TOK, TOK), TOK), pl.ds(0, TOK)]
        return (r_buf, k_buf)[a].at[at_block(me), :]

    def remote(a, d):
        t = partner(d)
        return pltpu.make_async_remote_copy(
            src_ref=source(a, t), dst_ref=target(a), send_sem=send_sem.at[a], recv_sem=recv_sem.at[a],
            device_id={"ctx": t}, device_id_type=MESH,
        )

    def all_of(a):
        rows = pl.ds(0, LENGTH - TOK)
        if a == 3:
            whole = segments.at[pl.ds(0, count - 1)]
        elif a == 2:
            whole = v_full.at[rows, pl.ds(0, TOK)]
        else:
            whole = (r_buf, k_buf)[a].at[rows, :]
        return pltpu.make_async_remote_copy(
            src_ref=whole, dst_ref=whole, send_sem=send_sem.at[a], recv_sem=recv_sem.at[a],
            device_id={"ctx": partner(1)}, device_id_type=MESH,
        )

    def query(d):
        t = partner(d)
        return pltpu.make_async_remote_copy(
            src_ref=q_in.at[0, :, at_block(t)], dst_ref=q_buf.at[at_block(me), :],
            send_sem=q_send, recv_sem=q_recv.at[d // 2], device_id={"ctx": t}, device_id_type=MESH,
        )

    def some_queries(n, rows):
        whole = q_buf.at[pl.ds(0, rows), :]
        return pltpu.make_async_remote_copy(
            src_ref=whole, dst_ref=whole, send_sem=q_send, recv_sem=q_recv.at[n],
            device_id={"ctx": partner(1)}, device_id_type=MESH,
        )

    def own(a):
        return pltpu.make_async_copy(source(a, me), target(a), own_sem.at[a])

    def own_query():
        return pltpu.make_async_copy(q_in.at[0, :, at_block(me)], q_buf.at[at_block(me), :], own_sem.at[4])

    def gain_copy():
        return pltpu.make_async_remote_copy(
            src_ref=gain_in, dst_ref=gains, send_sem=gain_send, recv_sem=gain_recv,
            device_id=crossed, device_id_type=MESH,
        )

    def each_partner(act):
        def one(d, carry):
            act(d)
            return carry

        lax.fori_loop(1, count, one, 0)

    def arrive(a):
        own(a).wait()
        all_of(a).wait_recv()

    barrier = pltpu.get_barrier_semaphore()

    @pl.when(away)
    def _():
        pl.semaphore_signal(barrier, inc=1, device_id=crossed, device_id_type=MESH)

    for d in range(1, count):
        pl.semaphore_signal(barrier, inc=1, device_id={"ctx": partner(d)}, device_id_type=MESH)
    for a in range(4):
        own(a).start()
    own_query().start()
    pl.semaphore_wait(barrier, jnp.where(away, count, count - 1))

    @pl.when(away)
    def _():
        gain_copy().start()

    @pl.when(jnp.logical_not(away))
    def _():
        pltpu.make_async_copy(gain_in, gains, gain_own).start()

    for a in (0, 3, 1, 2):
        each_partner(lambda d, a=a: remote(a, d).start())
    each_partner(lambda d: query(d).start())

    prepare_bands(k_full, v_full)
    arrive(0)
    merge_reflections(r_buf, y_buf)
    chain_blocks(r_buf, y_buf, w_buf)
    arrive(3)
    all_of(0).wait_send()
    place_documents(segments, q_full, k_full)
    arrive(1)
    all_of(3).wait_send()

    def put_query(b, rows):
        q_full[at_block(b), :TOK] = rows

    def put_key(b, rows):
        k_full[pl.ds(pl.multiple_of(BAND + b * TOK, TOK), TOK), :TOK] = rows

    def some_keys(g, carry):
        rotate([g * GROUP + u for u in range(GROUP)], k_buf, r_buf, w_buf, put_key)
        return carry

    lax.fori_loop(0, BLOCKS // GROUP, some_keys, 0)

    @pl.when(away)
    def _():
        gain_copy().wait()

    @pl.when(jnp.logical_not(away))
    def _():
        pltpu.make_async_copy(gain_in, gains, gain_own).wait()

    arrive(2)
    all_of(1).wait_send()

    def out_copy(t):
        return pltpu.make_async_remote_copy(
            src_ref=o_buf.at[at_block(t), :], dst_ref=out.at[0, :, at_block(me)],
            send_sem=out_send, recv_sem=out_recv, device_id={"ctx": t}, device_id_type=MESH,
        )

    def out_own_copy():
        return pltpu.make_async_copy(o_buf.at[at_block(me), :], out.at[0, :, at_block(me)], out_own)

    def attend(tile):
        rotate([2 * tile, 2 * tile + 1], q_buf, r_buf, w_buf, put_query)
        weigh(tile, q_full, k_full, s_buf, p_buf)
        mix(tile, p_buf, v_full, gains, o_buf)

    own_query().wait()
    some_queries(0, TOK).wait_recv()
    attend(pair)
    out_own_copy().start()
    out_copy(partner(1)).start()

    def finish(n, carry):
        tile = lax.rem(pair + tiles - n, tiles)
        some_queries(n, ROWS).wait_recv()
        attend(tile)
        for h in range(2):
            out_copy(2 * tile + h).start()
        return carry

    lax.fori_loop(1, tiles, finish, 0)

    all_of(2).wait_send()
    some_queries(0, LENGTH - TOK).wait_send()
    sent = o_buf.at[pl.ds(0, LENGTH - TOK), :]
    landed = out.at[0, :, pl.ds(0, LENGTH - TOK)]
    back = pltpu.make_async_remote_copy(
        src_ref=sent, dst_ref=landed, send_sem=out_send, recv_sem=out_recv,
        device_id={"ctx": partner(1)}, device_id_type=MESH,
    )
    back.wait_send()
    out_own_copy().wait()
    back.wait_recv()


def local(queries, key_rows, value_rows, reflections, segment_ids, head_gains):
    hbm = pl.BlockSpec(memory_space=pltpu.HBM)
    vmem = pl.BlockSpec(memory_space=pltpu.VMEM)
    dma = pltpu.SemaphoreType.DMA
    return pl.pallas_call(
        kernel,
        out_shape=pltpu.VMEM((1, TOK, HEADS * HD), BF16),
        in_specs=[hbm, hbm, hbm, hbm, vmem, vmem],
        out_specs=pl.BlockSpec(memory_space=pl.ANY),
        scratch_shapes=[
            pltpu.VMEM((LENGTH, HD), BF16),
            pltpu.VMEM((LENGTH, HD), BF16),
            pltpu.VMEM((LENGTH, HD), BF16),
            pltpu.VMEM((BAND + LENGTH, 2 * HD), BF16),
            pltpu.VMEM((BLOCKS, 1, TOK), jnp.int32),
            pltpu.VMEM((1, HD), F32),
            pltpu.VMEM((LENGTH, HD), F32),
            pltpu.VMEM((BLOCKS, 2 * HD, 2 * HD), BF16),
            pltpu.VMEM((LENGTH, 2 * HD), BF16),
            pltpu.VMEM((BAND + LENGTH, 2 * HD), BF16),
            pltpu.VMEM((ROWS, SPAN), F32),
            pltpu.VMEM((ROWS, SPAN), BF16),
            pltpu.VMEM((LENGTH, HD), BF16),
            dma((4,)),
            dma((4,)),
            dma((5,)),
            dma,
            dma((LENGTH // ROWS,)),
            dma,
            dma,
            dma,
            dma,
            dma,
            dma,
        ],
        compiler_params=pltpu.CompilerParams(
            collective_id=0, has_side_effects=True, vmem_limit_bytes=63 * 1024 * 1024
        ),
    )(queries, key_rows, value_rows, reflections, segment_ids, head_gains[None, :])


def solution(mesh):
    placed = (
        P("dp", "ctx", None),
        P("dp", "ctx", None),
        P("dp", "ctx", None),
        P("dp", "ctx", None),
        P("dp", "ctx"),
        P("dp"),
    )
    return jax.shard_map(
        local, mesh=mesh, in_specs=placed, out_specs=P("dp", "ctx", None), check_vma=False
    )
```

```python
import functools
import math

import jax
import jax.numpy as jnp
from jax import lax
from jax.experimental import pallas as pl
from jax.experimental.pallas import tpu as pltpu
from jax.sharding import PartitionSpec as P

HEADS = 16
HD = 128
TOK = 128
LENGTH = 2048
BAND = 1024
ROWS = 256
SPAN = BAND + ROWS
BLOCKS = LENGTH // TOK
GROUP = 4
EPSILON = 1e-06
TURNS = (2, 6, 1, 7, 3, 5, 4)
SENDS = (1,) + tuple(2 * n + e for n in TURNS for e in range(2))
FAR = 2.0**100
F32 = jnp.float32
BF16 = jnp.bfloat16
MESH = pl.DeviceIdType.MESH


def dot(a, b):
    return lax.dot_general(a, b, (((1,), (0,)), ((), ())), preferred_element_type=F32)


def dot_nt(a, b):
    return lax.dot_general(a, b, (((1,), (1,)), ((), ())), preferred_element_type=F32)


def dot_tn(a, b):
    return lax.dot_general(a, b, (((0,), (0,)), ((), ())), preferred_element_type=F32)


def halves(x):
    high = x.astype(BF16)
    return high, (x - high.astype(F32)).astype(BF16)


def beside(a, b):
    return jnp.concatenate([a, b], axis=1)


def below(a, b):
    return jnp.concatenate([a, b], axis=0)


def product(a_high, a_low, b_high, b_low):
    return dot(beside(a_high, a_low), below(b_high, b_high)) + dot(a_high, b_low)


def at_block(index, size=TOK):
    return pl.ds(pl.multiple_of(index * size, size), size)


def square_iota():
    i = lax.broadcasted_iota(jnp.int32, (TOK, TOK), 0)
    j = lax.broadcasted_iota(jnp.int32, (TOK, TOK), 1)
    return i, j


def merge_reflections(r_buf, y_buf):
    i, j = square_iota()
    apart = jnp.bitwise_xor(i, j)

    def group(g, carry):
        raws, merged, betas = [], [], []
        for u in range(GROUP):
            raw = r_buf[at_block(g * GROUP + u), :]
            wide = raw.astype(F32)
            beta = 2.0 / (jnp.sum(wide * wide, axis=1, keepdims=True) + EPSILON)
            raws.append(raw)
            betas.append(beta)
            merged.append(wide * beta)
        for level in range(7):
            chosen = (lax.shift_right_logical(apart, level) == 1) & (i > j)
            for u in range(GROUP):
                raw = raws[u]
                high, low = halves(merged[u])
                if level == 0:
                    cross = dot_nt(raw, raw) * betas[u]
                else:
                    cross = dot_nt(beside(high, low), beside(raw, raw))
                c_high, c_low = halves(jnp.where(chosen, cross, 0.0))
                merged[u] = merged[u] - product(c_high, c_low, high, low)
        for u in range(GROUP):
            y_buf[at_block(g * GROUP + u), :] = merged[u]
        return carry

    lax.fori_loop(0, BLOCKS // GROUP, group, 0)


def chain_blocks(r_buf, y_buf, w_buf):
    i, j = square_iota()

    def step(b, before):
        raw = r_buf[at_block(b), :]
        a_high, a_low = halves(before)
        y_high, y_low = halves(y_buf[at_block(b), :])
        z_high, z_low = halves(product(y_high, y_low, a_high, a_low))
        w_buf[b, :TOK, :TOK] = a_high
        w_buf[b, :TOK, TOK:] = a_low
        w_buf[b, TOK:, :TOK] = -z_high
        w_buf[b, TOK:, TOK:] = -z_low
        return before - dot_tn(below(raw, raw), below(z_high, z_low))

    lax.fori_loop(0, BLOCKS, step, jnp.where(i == j, 1.0, 0.0).astype(F32))


def rotate(blocks, x_buf, r_buf, w_buf, put):
    i, j = square_iota()
    for b in blocks:
        raw_x = x_buf[at_block(b), :]
        seen = jnp.where(i >= j, dot_nt(raw_x, r_buf[at_block(b), :]), 0.0)
        s_high, s_low = halves(seen)
        both = dot(beside(raw_x, s_high), w_buf[b])
        rest = dot(s_low, w_buf[b, TOK:, :TOK])
        put(b, (both[:, :TOK] + both[:, TOK:] + rest).astype(BF16))


def place_documents(segments, q_full, k_full):
    i, _ = square_iota()

    def one(b, carry):
        hot = jnp.where(segments[b] == i, 1.0, 0.0).astype(F32).T
        q_full[at_block(b), TOK:] = (hot * FAR).astype(BF16)
        k_full[pl.ds(pl.multiple_of(BAND + b * TOK, TOK), TOK), TOK:] = (hot - 1.0).astype(BF16)
        return carry

    lax.fori_loop(0, BLOCKS, one, 0)


def prepare_bands(k_full, v_full):
    k_full[:BAND, :TOK] = jnp.zeros((BAND, TOK), BF16)
    k_full[:BAND, TOK:] = jnp.full((BAND, TOK), -1.0, BF16)
    v_full[:BAND, :TOK] = jnp.zeros((BAND, TOK), BF16)
    v_full[:, TOK:] = jnp.ones((BAND + LENGTH, TOK), BF16)


def weigh(t, q_full, k_full, s_buf, p_buf):
    i = lax.broadcasted_iota(jnp.int32, (ROWS, ROWS), 0)
    j = lax.broadcasted_iota(jnp.int32, (ROWS, ROWS), 1)
    scale = math.log2(math.e) / math.sqrt(HD)
    q_rows = q_full[at_block(t, ROWS), :]
    most = None
    for n in range(SPAN // ROWS):
        keys = k_full[pl.ds(pl.multiple_of((t + n) * ROWS, ROWS), ROWS), :]
        scores = dot_nt(q_rows, keys)
        if n == SPAN // ROWS - 1:
            scores = jnp.where(i >= j, scores, -FAR)
        s_buf[:, n * ROWS : (n + 1) * ROWS] = scores
        folded = jnp.maximum(scores[:, :TOK], scores[:, TOK:])
        most = folded if most is None else jnp.maximum(most, folded)
    top = jnp.max(most, axis=1, keepdims=True)
    for n in range(SPAN // ROWS):
        piece = slice(n * ROWS, (n + 1) * ROWS)
        p_buf[:, piece] = jnp.exp2((s_buf[:, piece] - top) * scale).astype(BF16)


def mix(t, p_buf, v_full, gains, o_buf):
    both = dot(p_buf[...], v_full[pl.ds(pl.multiple_of(t * ROWS, ROWS), SPAN), :])
    o_buf[at_block(t, ROWS), :] = (both[:, :TOK] / both[:, TOK:] * gains[...]).astype(BF16)


def kernel(
    q_in, k_in, v_in, r_in, segment_in, gain_in, out,
    r_buf, q_buf, k_buf, v_full, segments, gains,
    y_buf, w_buf, q_full, k_full, s_buf, p_buf, o_buf,
    send_sem, recv_sem, own_sem, q_send, q_recv, out_send, out_recv, out_own, gain_send, gain_recv, gain_own,
):
    row, me = lax.axis_index("dp"), lax.axis_index("ctx")
    count = BLOCKS
    crossed = {"dp": me, "ctx": row}
    away = row != me

    tiles = LENGTH // ROWS
    pair, half = me // 2, lax.rem(me, 2)

    def partner(d):
        return 2 * lax.rem(pair + d // 2, tiles) + lax.rem(half + d, 2)

    def source(a, t):
        if a == 3:
            return segment_in
        return (r_in, k_in, v_in)[a].at[0, :, at_block(t)]

    def target(a):
        if a == 3:
            return segments.at[me]
        if a == 2:
            return v_full.at[pl.ds(pl.multiple_of(BAND + me * TOK, TOK), TOK), pl.ds(0, TOK)]
        return (r_buf, k_buf)[a].at[at_block(me), :]

    def remote(a, d):
        t = partner(d)
        return pltpu.make_async_remote_copy(
            src_ref=source(a, t), dst_ref=target(a), send_sem=send_sem.at[a], recv_sem=recv_sem.at[a],
            device_id={"ctx": t}, device_id_type=MESH,
        )

    def all_of(a):
        rows = pl.ds(0, LENGTH - TOK)
        if a == 3:
            whole = segments.at[pl.ds(0, count - 1)]
        elif a == 2:
            whole = v_full.at[rows, pl.ds(0, TOK)]
        else:
            whole = (r_buf, k_buf)[a].at[rows, :]
        return pltpu.make_async_remote_copy(
            src_ref=whole, dst_ref=whole, send_sem=send_sem.at[a], recv_sem=recv_sem.at[a],
            device_id={"ctx": partner(1)}, device_id_type=MESH,
        )

    def query(d):
        t = partner(d)
        return pltpu.make_async_remote_copy(
            src_ref=q_in.at[0, :, at_block(t)], dst_ref=q_buf.at[at_block(me), :],
            send_sem=q_send, recv_sem=q_recv.at[d // 2], device_id={"ctx": t}, device_id_type=MESH,
        )

    def some_queries(n, rows):
        whole = q_buf.at[pl.ds(0, rows), :]
        return pltpu.make_async_remote_copy(
            src_ref=whole, dst_ref=whole, send_sem=q_send, recv_sem=q_recv.at[n],
            device_id={"ctx": partner(1)}, device_id_type=MESH,
        )

    def own(a):
        return pltpu.make_async_copy(source(a, me), target(a), own_sem.at[a])

    def own_query():
        return pltpu.make_async_copy(q_in.at[0, :, at_block(me)], q_buf.at[at_block(me), :], own_sem.at[4])

    def gain_copy():
        return pltpu.make_async_remote_copy(
            src_ref=gain_in, dst_ref=gains, send_sem=gain_send, recv_sem=gain_recv,
            device_id=crossed, device_id_type=MESH,
        )

    def arrive(a):
        own(a).wait()
        all_of(a).wait_recv()

    barrier = pltpu.get_barrier_semaphore()

    @pl.when(away)
    def _():
        pl.semaphore_signal(barrier, inc=1, device_id=crossed, device_id_type=MESH)

    for d in range(1, count):
        pl.semaphore_signal(barrier, inc=1, device_id={"ctx": partner(d)}, device_id_type=MESH)
    for a in range(4):
        own(a).start()
    own_query().start()
    pl.semaphore_wait(barrier, jnp.where(away, count, count - 1))

    @pl.when(away)
    def _():
        gain_copy().start()

    @pl.when(jnp.logical_not(away))
    def _():
        pltpu.make_async_copy(gain_in, gains, gain_own).start()

    for a in (0, 3, 1, 2):
        for d in SENDS:
            remote(a, d).start()
    for d in SENDS:
        query(d).start()

    prepare_bands(k_full, v_full)
    arrive(0)
    merge_reflections(r_buf, y_buf)
    chain_blocks(r_buf, y_buf, w_buf)
    arrive(3)
    all_of(0).wait_send()
    place_documents(segments, q_full, k_full)
    arrive(1)
    all_of(3).wait_send()

    def put_query(b, rows):
        q_full[at_block(b), :TOK] = rows

    def put_key(b, rows):
        k_full[pl.ds(pl.multiple_of(BAND + b * TOK, TOK), TOK), :TOK] = rows

    def some_keys(g, carry):
        rotate([g * GROUP + u for u in range(GROUP)], k_buf, r_buf, w_buf, put_key)
        return carry

    lax.fori_loop(0, BLOCKS // GROUP, some_keys, 0)

    @pl.when(away)
    def _():
        gain_copy().wait()

    @pl.when(jnp.logical_not(away))
    def _():
        pltpu.make_async_copy(gain_in, gains, gain_own).wait()

    arrive(2)
    all_of(1).wait_send()

    def out_copy(t):
        return pltpu.make_async_remote_copy(
            src_ref=o_buf.at[at_block(t), :], dst_ref=out.at[0, :, at_block(me)],
            send_sem=out_send, recv_sem=out_recv, device_id={"ctx": t}, device_id_type=MESH,
        )

    def out_own_copy():
        return pltpu.make_async_copy(o_buf.at[at_block(me), :], out.at[0, :, at_block(me)], out_own)

    def attend(tile):
        rotate([2 * tile, 2 * tile + 1], q_buf, r_buf, w_buf, put_query)
        weigh(tile, q_full, k_full, s_buf, p_buf)
        mix(tile, p_buf, v_full, gains, o_buf)

    own_query().wait()
    some_queries(0, TOK).wait_recv()
    attend(pair)
    out_own_copy().start()
    out_copy(partner(1)).start()

    def finish(turn, carry):
        n = TURNS[turn - 1]
        tile = lax.rem(pair + tiles - n, tiles)
        some_queries(n, ROWS).wait_recv()
        attend(tile)
        for h in range(2):
            out_copy(2 * tile + h).start()
        return carry

    for turn in range(1, tiles):
        finish(turn, 0)

    all_of(2).wait_send()
    some_queries(0, LENGTH - TOK).wait_send()
    sent = o_buf.at[pl.ds(0, LENGTH - TOK), :]
    landed = out.at[0, :, pl.ds(0, LENGTH - TOK)]
    back = pltpu.make_async_remote_copy(
        src_ref=sent, dst_ref=landed, send_sem=out_send, recv_sem=out_recv,
        device_id={"ctx": partner(1)}, device_id_type=MESH,
    )
    back.wait_send()
    out_own_copy().wait()
    back.wait_recv()


def local(queries, key_rows, value_rows, reflections, segment_ids, head_gains):
    hbm = pl.BlockSpec(memory_space=pltpu.HBM)
    vmem = pl.BlockSpec(memory_space=pltpu.VMEM)
    dma = pltpu.SemaphoreType.DMA
    return pl.pallas_call(
        kernel,
        out_shape=pltpu.VMEM((1, TOK, HEADS * HD), BF16),
        in_specs=[hbm, hbm, hbm, hbm, vmem, vmem],
        out_specs=pl.BlockSpec(memory_space=pl.ANY),
        scratch_shapes=[
            pltpu.VMEM((LENGTH, HD), BF16),
            pltpu.VMEM((LENGTH, HD), BF16),
            pltpu.VMEM((LENGTH, HD), BF16),
            pltpu.VMEM((BAND + LENGTH, 2 * HD), BF16),
            pltpu.VMEM((BLOCKS, 1, TOK), jnp.int32),
            pltpu.VMEM((1, HD), F32),
            pltpu.VMEM((LENGTH, HD), F32),
            pltpu.VMEM((BLOCKS, 2 * HD, 2 * HD), BF16),
            pltpu.VMEM((LENGTH, 2 * HD), BF16),
            pltpu.VMEM((BAND + LENGTH, 2 * HD), BF16),
            pltpu.VMEM((ROWS, SPAN), F32),
            pltpu.VMEM((ROWS, SPAN), BF16),
            pltpu.VMEM((LENGTH, HD), BF16),
            dma((4,)),
            dma((4,)),
            dma((5,)),
            dma,
            dma((LENGTH // ROWS,)),
            dma,
            dma,
            dma,
            dma,
            dma,
            dma,
        ],
        compiler_params=pltpu.CompilerParams(
            collective_id=0, has_side_effects=True, vmem_limit_bytes=63 * 1024 * 1024
        ),
    )(queries, key_rows, value_rows, reflections, segment_ids, head_gains[None, :])


def solution(mesh):
    placed = (
        P("dp", "ctx", None),
        P("dp", "ctx", None),
        P("dp", "ctx", None),
        P("dp", "ctx", None),
        P("dp", "ctx"),
        P("dp"),
    )
    return jax.shard_map(
        local, mesh=mesh, in_specs=placed, out_specs=P("dp", "ctx", None), check_vma=False
    )
```

```python
import functools
import math

import jax
import jax.numpy as jnp
from jax import lax
from jax.experimental import pallas as pl
from jax.experimental.pallas import tpu as pltpu
from jax.sharding import PartitionSpec as P

HEADS = 16
HD = 128
TOK = 128
LENGTH = 2048
BAND = 1024
ROWS = 256
SPAN = BAND + ROWS
BLOCKS = LENGTH // TOK
GROUP = 4
EPSILON = 1e-06
TURNS = (2, 6, 1, 7, 3, 5, 4)
SENDS = (1,) + tuple(2 * n + e for n in TURNS for e in range(2))
FAR = 2.0**100
F32 = jnp.float32
BF16 = jnp.bfloat16
MESH = pl.DeviceIdType.MESH


def dot(a, b):
    return lax.dot_general(a, b, (((1,), (0,)), ((), ())), preferred_element_type=F32)


def dot_nt(a, b):
    return lax.dot_general(a, b, (((1,), (1,)), ((), ())), preferred_element_type=F32)


def dot_tn(a, b):
    return lax.dot_general(a, b, (((0,), (0,)), ((), ())), preferred_element_type=F32)


def halves(x):
    high = x.astype(BF16)
    return high, (x - high.astype(F32)).astype(BF16)


def beside(a, b):
    return jnp.concatenate([a, b], axis=1)


def below(a, b):
    return jnp.concatenate([a, b], axis=0)


def product(a_high, a_low, b_high, b_low):
    return dot(beside(a_high, a_low), below(b_high, b_high)) + dot(a_high, b_low)


def at_block(index, size=TOK):
    return pl.ds(pl.multiple_of(index * size, size), size)


def square_iota():
    i = lax.broadcasted_iota(jnp.int32, (TOK, TOK), 0)
    j = lax.broadcasted_iota(jnp.int32, (TOK, TOK), 1)
    return i, j


def merge_reflections(r_buf, y_buf):
    i, j = square_iota()
    apart = jnp.bitwise_xor(i, j)

    def group(g, carry):
        raws, merged, betas = [], [], []
        for u in range(GROUP):
            raw = r_buf[at_block(g * GROUP + u), :]
            wide = raw.astype(F32)
            beta = 2.0 / (jnp.sum(wide * wide, axis=1, keepdims=True) + EPSILON)
            raws.append(raw)
            betas.append(beta)
            merged.append(wide * beta)
        for level in range(7):
            chosen = (lax.shift_right_logical(apart, level) == 1) & (i > j)
            for u in range(GROUP):
                raw = raws[u]
                high, low = halves(merged[u])
                if level == 0:
                    cross = dot_nt(raw, raw) * betas[u]
                else:
                    cross = dot_nt(beside(high, low), beside(raw, raw))
                c_high, c_low = halves(jnp.where(chosen, cross, 0.0))
                merged[u] = merged[u] - product(c_high, c_low, high, low)
        for u in range(GROUP):
            y_buf[at_block(g * GROUP + u), :] = merged[u]
        return carry

    lax.fori_loop(0, BLOCKS // GROUP, group, 0)


def chain_blocks(r_buf, y_buf, w_buf):
    i, j = square_iota()

    def step(b, before):
        raw = r_buf[at_block(b), :]
        a_high, a_low = halves(before)
        y_high, y_low = halves(y_buf[at_block(b), :])
        z_high, z_low = halves(product(y_high, y_low, a_high, a_low))
        w_buf[b, :TOK, :TOK] = a_high
        w_buf[b, :TOK, TOK:] = a_low
        w_buf[b, TOK:, :TOK] = -z_high
        w_buf[b, TOK:, TOK:] = -z_low
        return before - dot_tn(below(raw, raw), below(z_high, z_low))

    lax.fori_loop(0, BLOCKS, step, jnp.where(i == j, 1.0, 0.0).astype(F32))


def rotate(blocks, x_buf, r_buf, w_buf, put):
    i, j = square_iota()
    for b in blocks:
        raw_x = x_buf[at_block(b), :]
        seen = jnp.where(i >= j, dot_nt(raw_x, r_buf[at_block(b), :]), 0.0)
        s_high, s_low = halves(seen)
        both = dot(beside(raw_x, s_high), w_buf[b])
        rest = dot(s_low, w_buf[b, TOK:, :TOK])
        put(b, (both[:, :TOK] + both[:, TOK:] + rest).astype(BF16))


def place_documents(segments, q_full, k_full):
    i, _ = square_iota()

    def one(b, carry):
        hot = jnp.where(segments[b] == i, 1.0, 0.0).astype(F32).T
        q_full[at_block(b), TOK:] = (hot * FAR).astype(BF16)
        k_full[pl.ds(pl.multiple_of(BAND + b * TOK, TOK), TOK), TOK:] = (hot - 1.0).astype(BF16)
        return carry

    lax.fori_loop(0, BLOCKS, one, 0)


def prepare_bands(k_full, v_full):
    k_full[:BAND, :TOK] = jnp.zeros((BAND, TOK), BF16)
    k_full[:BAND, TOK:] = jnp.full((BAND, TOK), -1.0, BF16)
    v_full[:BAND, :TOK] = jnp.zeros((BAND, TOK), BF16)
    v_full[:, TOK:] = jnp.ones((BAND + LENGTH, TOK), BF16)


def weigh(t, q_full, k_full, s_buf, p_buf):
    i = lax.broadcasted_iota(jnp.int32, (ROWS, ROWS), 0)
    j = lax.broadcasted_iota(jnp.int32, (ROWS, ROWS), 1)
    scale = math.log2(math.e) / math.sqrt(HD)
    q_rows = q_full[at_block(t, ROWS), :]
    most = None
    for n in range(SPAN // ROWS):
        keys = k_full[pl.ds(pl.multiple_of((t + n) * ROWS, ROWS), ROWS), :]
        scores = dot_nt(q_rows, keys)
        if n == SPAN // ROWS - 1:
            scores = jnp.where(i >= j, scores, -FAR)
        s_buf[:, n * ROWS : (n + 1) * ROWS] = scores
        folded = jnp.maximum(scores[:, :TOK], scores[:, TOK:])
        most = folded if most is None else jnp.maximum(most, folded)
    top = jnp.max(most, axis=1, keepdims=True)
    for n in range(SPAN // ROWS):
        piece = slice(n * ROWS, (n + 1) * ROWS)
        p_buf[:, piece] = jnp.exp2((s_buf[:, piece] - top) * scale).astype(BF16)


def mix(t, p_buf, v_full, gains, o_buf):
    both = dot(p_buf[...], v_full[pl.ds(pl.multiple_of(t * ROWS, ROWS), SPAN), :])
    o_buf[at_block(t, ROWS), :] = (both[:, :TOK] / both[:, TOK:] * gains[...]).astype(BF16)


def kernel(
    q_in, k_in, v_in, r_in, segment_in, gain_in, out,
    r_buf, q_buf, k_buf, v_full, segments, gains,
    y_buf, w_buf, q_full, k_full, s_buf, p_buf, o_buf,
    send_sem, recv_sem, own_sem, q_send, q_recv, out_send, out_recv, out_own, gain_send, gain_recv, gain_own,
):
    row, me = lax.axis_index("dp"), lax.axis_index("ctx")
    count = BLOCKS
    crossed = {"dp": me, "ctx": row}
    away = row != me

    tiles = LENGTH // ROWS
    pair, half = me // 2, lax.rem(me, 2)

    def partner(d):
        return 2 * lax.rem(pair + d // 2, tiles) + lax.rem(half + d, 2)

    def source(a, t):
        if a == 3:
            return segment_in
        return (r_in, k_in, v_in)[a].at[0, :, at_block(t)]

    def target(a):
        if a == 3:
            return segments.at[me]
        if a == 2:
            return v_full.at[pl.ds(pl.multiple_of(BAND + me * TOK, TOK), TOK), pl.ds(0, TOK)]
        return (r_buf, k_buf)[a].at[at_block(me), :]

    def remote(a, d):
        t = partner(d)
        return pltpu.make_async_remote_copy(
            src_ref=source(a, t), dst_ref=target(a), send_sem=send_sem.at[a], recv_sem=recv_sem.at[a],
            device_id={"ctx": t}, device_id_type=MESH,
        )

    def all_of(a):
        rows = pl.ds(0, LENGTH - TOK)
        if a == 3:
            whole = segments.at[pl.ds(0, count - 1)]
        elif a == 2:
            whole = v_full.at[rows, pl.ds(0, TOK)]
        else:
            whole = (r_buf, k_buf)[a].at[rows, :]
        return pltpu.make_async_remote_copy(
            src_ref=whole, dst_ref=whole, send_sem=send_sem.at[a], recv_sem=recv_sem.at[a],
            device_id={"ctx": partner(1)}, device_id_type=MESH,
        )

    def query(d):
        t = partner(d)
        return pltpu.make_async_remote_copy(
            src_ref=q_in.at[0, :, at_block(t)], dst_ref=q_buf.at[at_block(me), :],
            send_sem=q_send, recv_sem=q_recv.at[d // 2], device_id={"ctx": t}, device_id_type=MESH,
        )

    def some_queries(n, rows):
        whole = q_buf.at[pl.ds(0, rows), :]
        return pltpu.make_async_remote_copy(
            src_ref=whole, dst_ref=whole, send_sem=q_send, recv_sem=q_recv.at[n],
            device_id={"ctx": partner(1)}, device_id_type=MESH,
        )

    def own(a):
        return pltpu.make_async_copy(source(a, me), target(a), own_sem.at[a])

    def own_query():
        return pltpu.make_async_copy(q_in.at[0, :, at_block(me)], q_buf.at[at_block(me), :], own_sem.at[4])

    def gain_copy():
        return pltpu.make_async_remote_copy(
            src_ref=gain_in, dst_ref=gains, send_sem=gain_send, recv_sem=gain_recv,
            device_id=crossed, device_id_type=MESH,
        )

    def arrive(a):
        own(a).wait()
        all_of(a).wait_recv()

    barrier = pltpu.get_barrier_semaphore()

    @pl.when(away)
    def _():
        pl.semaphore_signal(barrier, inc=1, device_id=crossed, device_id_type=MESH)

    for d in SENDS[1:] + SENDS[:1]:
        pl.semaphore_signal(barrier, inc=1, device_id={"ctx": partner(d)}, device_id_type=MESH)
    for a in range(4):
        own(a).start()
    own_query().start()
    pl.semaphore_wait(barrier, jnp.where(away, count, count - 1))

    @pl.when(away)
    def _():
        gain_copy().start()

    @pl.when(jnp.logical_not(away))
    def _():
        pltpu.make_async_copy(gain_in, gains, gain_own).start()

    for a in (0, 3, 1, 2):
        for d in SENDS:
            remote(a, d).start()
    for d in SENDS:
        query(d).start()

    prepare_bands(k_full, v_full)
    arrive(0)
    merge_reflections(r_buf, y_buf)
    chain_blocks(r_buf, y_buf, w_buf)
    arrive(3)
    all_of(0).wait_send()
    place_documents(segments, q_full, k_full)
    arrive(1)
    all_of(3).wait_send()

    def put_query(b, rows):
        q_full[at_block(b), :TOK] = rows

    def put_key(b, rows):
        k_full[pl.ds(pl.multiple_of(BAND + b * TOK, TOK), TOK), :TOK] = rows

    def some_keys(g, carry):
        rotate([g * GROUP + u for u in range(GROUP)], k_buf, r_buf, w_buf, put_key)
        return carry

    lax.fori_loop(0, BLOCKS // GROUP, some_keys, 0)

    @pl.when(away)
    def _():
        gain_copy().wait()

    @pl.when(jnp.logical_not(away))
    def _():
        pltpu.make_async_copy(gain_in, gains, gain_own).wait()

    arrive(2)
    all_of(1).wait_send()

    def out_copy(t):
        return pltpu.make_async_remote_copy(
            src_ref=o_buf.at[at_block(t), :], dst_ref=out.at[0, :, at_block(me)],
            send_sem=out_send, recv_sem=out_recv, device_id={"ctx": t}, device_id_type=MESH,
        )

    def out_own_copy():
        return pltpu.make_async_copy(o_buf.at[at_block(me), :], out.at[0, :, at_block(me)], out_own)

    def attend(tile):
        rotate([2 * tile, 2 * tile + 1], q_buf, r_buf, w_buf, put_query)
        weigh(tile, q_full, k_full, s_buf, p_buf)
        mix(tile, p_buf, v_full, gains, o_buf)

    own_query().wait()
    some_queries(0, TOK).wait_recv()
    attend(pair)
    out_own_copy().start()
    out_copy(partner(1)).start()

    def finish(turn, carry):
        n = TURNS[turn - 1]
        tile = lax.rem(pair + tiles - n, tiles)
        some_queries(n, ROWS).wait_recv()
        attend(tile)
        for h in range(2):
            out_copy(2 * tile + h).start()
        return carry

    for turn in range(1, tiles):
        finish(turn, 0)

    all_of(2).wait_send()
    some_queries(0, LENGTH - TOK).wait_send()
    sent = o_buf.at[pl.ds(0, LENGTH - TOK), :]
    landed = out.at[0, :, pl.ds(0, LENGTH - TOK)]
    back = pltpu.make_async_remote_copy(
        src_ref=sent, dst_ref=landed, send_sem=out_send, recv_sem=out_recv,
        device_id={"ctx": partner(1)}, device_id_type=MESH,
    )
    back.wait_send()
    out_own_copy().wait()
    back.wait_recv()


def local(queries, key_rows, value_rows, reflections, segment_ids, head_gains):
    hbm = pl.BlockSpec(memory_space=pltpu.HBM)
    vmem = pl.BlockSpec(memory_space=pltpu.VMEM)
    dma = pltpu.SemaphoreType.DMA
    return pl.pallas_call(
        kernel,
        out_shape=pltpu.VMEM((1, TOK, HEADS * HD), BF16),
        in_specs=[hbm, hbm, hbm, hbm, vmem, vmem],
        out_specs=pl.BlockSpec(memory_space=pl.ANY),
        scratch_shapes=[
            pltpu.VMEM((LENGTH, HD), BF16),
            pltpu.VMEM((LENGTH, HD), BF16),
            pltpu.VMEM((LENGTH, HD), BF16),
            pltpu.VMEM((BAND + LENGTH, 2 * HD), BF16),
            pltpu.VMEM((BLOCKS, 1, TOK), jnp.int32),
            pltpu.VMEM((1, HD), F32),
            pltpu.VMEM((LENGTH, HD), F32),
            pltpu.VMEM((BLOCKS, 2 * HD, 2 * HD), BF16),
            pltpu.VMEM((LENGTH, 2 * HD), BF16),
            pltpu.VMEM((BAND + LENGTH, 2 * HD), BF16),
            pltpu.VMEM((ROWS, SPAN), F32),
            pltpu.VMEM((ROWS, SPAN), BF16),
            pltpu.VMEM((LENGTH, HD), BF16),
            dma((4,)),
            dma((4,)),
            dma((5,)),
            dma,
            dma((LENGTH // ROWS,)),
            dma,
            dma,
            dma,
            dma,
            dma,
            dma,
        ],
        compiler_params=pltpu.CompilerParams(
            collective_id=0, has_side_effects=True, vmem_limit_bytes=63 * 1024 * 1024
        ),
    )(queries, key_rows, value_rows, reflections, segment_ids, head_gains[None, :])


def solution(mesh):
    placed = (
        P("dp", "ctx", None),
        P("dp", "ctx", None),
        P("dp", "ctx", None),
        P("dp", "ctx", None),
        P("dp", "ctx"),
        P("dp"),
    )
    return jax.shard_map(
        local, mesh=mesh, in_specs=placed, out_specs=P("dp", "ctx", None), check_vma=False
    )
```
